32 devices in a mesh: section: 4 (over x, core), tp: 4 (over z), cfg: 2 (over y).
Axes of the slice: x: 2, y: 2, z: 4, core: 2. Of those that a mesh axis runs over, the one named last changes fastest.
Arguments:
- inflow: bfloat16 [4, 512, 3072], P('section', 'cfg', 'tp'), parts along dimension 1, may hold values from -6 to 6
- w_qkv: bfloat16 [4, 3072, 3, 2048], P('section', None, None, 'tp'), may hold values from -0.109375 to 0.109375
- w_out: bfloat16 [4, 2048, 3072], P('section', 'tp'), may hold values from -0.125 to 0.125
- mod_shift: float32 [4, 3072], P('section'), may hold values from -3 to 3
- mod_scale: float32 [4, 3072], P('section'), may hold values from -1.5 to 1.5
- mod_gate: float32 [4, 3072], P('section'), may hold values from 0.5 to 1.5
- q_gain: float32 [4, 128], P('section'), may hold values from 1.5 to 4
- k_gain: float32 [4, 128], P('section'), may hold values from 0.5 to 1.5
- kv_cache: bfloat16 [4, 2048, 2, 2048], P('section', 'cfg', None, 'tp'), parts along dimension 1, may hold values from -6 to 6
- patch_id: int32 [2, 4], replicated, may hold values from 0 to 3, as said below
- positions: int32 [4, 256], replicated, may hold values from 0 to 1023, as said below
Outputs:
- outflow: bfloat16 [4, 512, 3072], P('section', 'cfg', 'tp'), parts along dimension 1
The draws below stay inside these ranges and needn't reach their ends.
There are 2 independent parts, one for each index of `cfg`. The reference program is written for one: setup_inputs(seed, part) draws one part's arguments, and reference() takes and returns one part's arrays. A program takes and returns all parts, laid end to end along the dimension named above; an argument that names none is the same for every part. Nothing has to cross between parts.
Inputs may be any that keep to these rules, and one draw needn't show every extreme that they name: patch_id[t, s] = patch_id[t - 1, s - 1] with s - 1 taken modulo 4; each row names every patch once. `positions`: every token position stands exactly once.
All inputs are finite; a program needn't handle non-finite values.
Results may differ from the reference program's by a relative error of at most 0.015.
Values may be sent and summed in bfloat16 or wider, within the bound.
A program may use at most 128 MiB of HBM per device.

```python
import math
import jax
import jax.numpy as jnp
from jax import lax

D = 3072
HEADS = 16
HD = 128
PATCH = 256
TICKS = 2
PATCHES = 4
TOKENS = 1024
N_SECTION = 4
N_TP = 4


def draw_patch_id(key, part):
    order = jax.random.permutation(jax.random.fold_in(key, 11), PATCHES).astype(jnp.int32)
    column = jnp.arange(PATCHES, dtype=jnp.int32)[None, :]
    ticked = jnp.arange(TICKS, dtype=jnp.int32)[:, None]
    return order[(column - ticked) % PATCHES].astype(jnp.int32)


def draw_positions(key, part):
    order = jax.random.permutation(jax.random.fold_in(key, 23), TOKENS).astype(jnp.int32)
    return order.reshape(PATCHES, PATCH)


def steps_of(rng, dims, pieces, least, largest):
    factor_of = 1.0
    for axis_at, blocks in pieces:
        steps = jax.random.uniform(jax.random.fold_in(jax.random.fold_in(rng, 6), axis_at), (blocks,), jnp.float32, least / len(pieces), largest / len(pieces))
        factor_of = factor_of * jnp.repeat(jnp.exp(steps), dims[axis_at] // blocks).reshape((-1,) + (1,) * (len(dims) - 1 - axis_at))
    return factor_of


def gaussian(rng, shape, scale, limit, split=(), held_as=jnp.bfloat16):
    drawn = jax.random.normal(rng, shape, jnp.float32) * scale
    if len(split) > 0:
        drawn = steps_of(rng, shape, split, -0.22, 0.18) * drawn
    return jnp.clip(drawn, min=-limit, max=limit).astype(held_as)


def setup_inputs(seed: int = 0, part: int = 0) -> dict:
    arg_keys = jax.random.split(jax.random.key(seed), 12)
    own_keys = jax.random.split(jax.random.fold_in(arg_keys[11], part), 12)
    return {
        "inflow": gaussian(own_keys[0], (N_SECTION, PATCH, D), 1.0, 6.0, ((0, 4), (2, 4))),
        "w_qkv": gaussian(arg_keys[1], (N_SECTION, D, 3, HEADS * HD), D ** -0.5, 0.109375, ((0, 4), (3, 4))),
        "w_out": gaussian(arg_keys[2], (N_SECTION, HEADS * HD, D), (HEADS * HD) ** -0.5, 0.125, ((0, 4), (1, 4))),
        "mod_shift": gaussian(arg_keys[3], (N_SECTION, D), 0.5, 3.0, ((0, 4),), jnp.float32),
        "mod_scale": gaussian(arg_keys[4], (N_SECTION, D), 0.3, 1.5, ((0, 4),), jnp.float32),
        "mod_gate": jnp.clip(0.5 + 1.0 * jax.random.uniform(arg_keys[5], (N_SECTION, D), jnp.float32) ** steps_of(arg_keys[5], (N_SECTION, D), ((0, 4),), -0.2, 0.2), 0.5, 1.5),
        "q_gain": jnp.clip(jnp.exp(math.log(4.0) - 0.98082925 * jax.random.uniform(arg_keys[6], (N_SECTION, HD), jnp.float32) ** steps_of(arg_keys[6], (N_SECTION, HD), ((0, 4),), -0.2, 0.2)), 1.5, 4.0),
        "k_gain": jnp.clip(1.0 + 0.1 * jax.random.normal(arg_keys[7], (N_SECTION, HD), jnp.float32), 0.5, 1.5),
        "kv_cache": gaussian(own_keys[8], (N_SECTION, TOKENS, 2, HEADS * HD), 1.0, 6.0, ((0, 4), (3, 4))),
        "patch_id": draw_patch_id(jax.random.fold_in(arg_keys[11], 71), part),
        "positions": draw_positions(jax.random.fold_in(arg_keys[11], 71), part),
    }


def rms_scale(values, gain):
    moment = lax.optimization_barrier(jnp.mean(values * values, axis=-1, keepdims=True))
    return values * lax.rsqrt(moment + jnp.float32(1e-06)) * gain

def one_block(state, w_qkv, w_out, mod_shift, mod_scale, mod_gate, q_gain, k_gain, kv_cache, patch_no, positions):
    state_f = state.astype(jnp.float32)
    center = lax.optimization_barrier(jnp.mean(state_f, axis=-1, keepdims=True))
    varied = lax.optimization_barrier(jnp.mean((state_f - center) * (state_f - center), axis=-1, keepdims=True))
    normed = ((state_f - center) * lax.rsqrt(varied + 1e-06) * (1.0 + mod_scale) + mod_shift).astype(jnp.bfloat16)
    fresh = jnp.dot(normed, w_qkv.reshape(D, 3 * HEADS * HD), preferred_element_type=jnp.float32)
    fresh = fresh.astype(jnp.bfloat16).reshape(PATCH, 3, HEADS * HD)
    rows_at = lax.dynamic_index_in_dim(positions, patch_no, 0, keepdims=False).astype(jnp.int32)
    updated = kv_cache.at[rows_at].set(fresh[:, 1:])
    queries = rms_scale(fresh[:, 0].astype(jnp.float32).reshape(PATCH, HEADS, HD), q_gain).astype(jnp.bfloat16)
    keys_n = rms_scale(updated[:, 0].astype(jnp.float32).reshape(TOKENS, HEADS, HD), k_gain).astype(jnp.bfloat16)
    values_v = updated[:, 1].reshape(TOKENS, HEADS, HD)
    scores = jnp.einsum('phd,thd->hpt', queries.astype(jnp.float32), keys_n.astype(jnp.float32)) * HD ** (-0.5)
    expon = jnp.exp(scores)
    attn_probs = (expon / lax.optimization_barrier(jnp.sum(expon, axis=-1, keepdims=True))).astype(jnp.bfloat16)
    mixed = jnp.einsum('hpt,thd->phd', attn_probs.astype(jnp.float32), values_v.astype(jnp.float32))
    mixed = mixed.astype(jnp.bfloat16).reshape(PATCH, N_TP, HEADS * HD // N_TP)
    out_rows = w_out.reshape(N_TP, HEADS * HD // N_TP, D)
    partial_value = jnp.einsum('pgh,ghd->gpd', mixed.astype(jnp.float32), out_rows.astype(jnp.float32)).astype(jnp.bfloat16)
    summed = lax.optimization_barrier(jnp.sum(partial_value.astype(jnp.float32), axis=0))
    result = (state_f + mod_gate * summed).astype(jnp.bfloat16)
    return (result, updated)

def reference(inflow, w_qkv, w_out, mod_shift, mod_scale, mod_gate, q_gain, k_gain, kv_cache, patch_id, positions):
    states = inflow
    caches = kv_cache
    results = inflow
    for tick_no in range(TICKS):

        def section_step(items):
            return one_block(*items, positions)
        results, caches = lax.map(section_step, (states, w_qkv, w_out, mod_shift, mod_scale, mod_gate, q_gain, k_gain, caches, patch_id[tick_no]))
        if tick_no + 1 < TICKS:
            states = jnp.roll(results, 1, axis=0)
    return results
```

```python
import functools

import jax
import jax.numpy as jnp
from jax import lax
from jax.experimental import pallas as pl
from jax.experimental.pallas import tpu as pltpu
from jax.sharding import PartitionSpec as P

HD = 128
TICKS = 2
CHUNKS = 4
MESH = pl.DeviceIdType.MESH
F32 = jnp.float32
BF16 = jnp.bfloat16


def head_norm(values, gain):
    moment = jnp.mean(values * values, axis=-1, keepdims=True)
    return (values * lax.rsqrt(moment + 1e-06) * gain).astype(BF16)


def kernel(
    n,
    sections,
    x_ref,
    wq_hbm,
    wo_hbm,
    shift_ref,
    scale_ref,
    gate_ref,
    qg_ref,
    kg_ref,
    kv_hbm,
    mask_ref,
    out_ref,
    xg,
    wq,
    wo,
    kvb,
    keys,
    vals,
    normed,
    queries,
    mixed,
    part,
    from_left,
    from_right,
    acc,
    local_sem,
    ag_send,
    ag_recv,
    rs_send,
    rs_left,
    rs_right,
    sec_send,
    sec_recv,
):
    me = lax.axis_index("tp")
    sec = lax.axis_index("section")
    after, before = lax.rem(sec + 1, sections), lax.rem(sec + sections - 1, sections)
    rows_all, share = x_ref.shape
    width = n * share
    tokens = kvb.shape[0]
    head_cols = wo.shape[0]
    size = rows_all // CHUNKS

    load_kv = pltpu.make_async_copy(kv_hbm, kvb, local_sem.at[0])
    load_wq = pltpu.make_async_copy(wq_hbm, wq, local_sem.at[1])
    load_wo = pltpu.make_async_copy(wo_hbm, wo, local_sem.at[2])
    load_kv.start()
    load_wq.start()
    load_wo.start()

    barrier = pltpu.get_barrier_semaphore()
    pl.semaphore_signal(barrier, inc=1, device_id={"section": after}, device_id_type=MESH)
    pl.semaphore_signal(barrier, inc=1, device_id={"section": before}, device_id_type=MESH)

    @pl.when(me > 0)
    def _():
        pl.semaphore_signal(barrier, inc=1, device_id={"tp": me - 1}, device_id_type=MESH)

    @pl.when(me < n - 1)
    def _():
        pl.semaphore_signal(barrier, inc=1, device_id={"tp": me + 1}, device_id_type=MESH)

    pl.semaphore_wait(barrier, 2 + jnp.minimum(me, 1) + jnp.minimum(n - 1 - me, 1))

    def rows(c):
        return pl.ds(c * size, size)

    def ag_copy(tick, way, step, c):
        shard = me - step if way == 0 else me + step
        here = xg.at[tick, shard, rows(c)]
        source = x_ref.at[rows(c)] if tick == 0 and step == 0 else here
        return pltpu.make_async_remote_copy(
            src_ref=source,
            dst_ref=here,
            send_sem=ag_send.at[tick, way, step, c],
            recv_sem=ag_recv.at[tick, shard, c],
            device_id={"tp": me + 1 if way == 0 else me - 1},
            device_id_type=MESH,
        )

    def ag_when(way, step):
        held = me - step >= 0 if way == 0 else me + step <= n - 1
        onward = me < n - 1 if way == 0 else me > 0
        return held, onward

    def ag_own(tick, c):
        for way in range(2):
            _, onward = ag_when(way, 0)

            @pl.when(onward)
            def _():
                ag_copy(tick, way, 0, c).start()

    def ag_relay(tick, c, step):
        for way in range(2):
            held, onward = ag_when(way, step)

            @pl.when(held)
            def _():
                ag_copy(tick, way, step, c).wait_recv()

                @pl.when(onward)
                def _():
                    ag_copy(tick, way, step, c).start()

    def ag_drain(tick, c):
        for step in range(n - 1):
            for way in range(2):
                held, onward = ag_when(way, step)

                @pl.when(held & onward)
                def _():
                    ag_copy(tick, way, step, c).wait_send()

    def rs_copy(tick, way, shard, c):
        landing, sems = (from_left, rs_left) if way == 0 else (from_right, rs_right)
        return pltpu.make_async_remote_copy(
            src_ref=part.at[shard, rows(c)],
            dst_ref=landing.at[tick, shard, rows(c)],
            send_sem=rs_send.at[tick, shard, c],
            recv_sem=sems.at[tick, shard, c],
            device_id={"tp": me + 1 if way == 0 else me - 1},
            device_id_type=MESH,
        )

    def rs_first(tick, c):
        @pl.when(me == 0)
        def _():
            for shard in range(n - 1, 0, -1):
                rs_copy(tick, 0, shard, c).start()

        @pl.when(me == n - 1)
        def _():
            for shard in range(n - 1):
                rs_copy(tick, 1, shard, c).start()

    def rs_rest(tick, c):
        for away in range(n - 1):
            far, near = n - 1 - away, away

            @pl.when((me > 0) & (me < far))
            def _():
                rs_copy(tick, 0, far, c).wait_recv()
                part[far, rows(c)] = (
                    part[far, rows(c)].astype(F32) + from_left[tick, far, rows(c)].astype(F32)
                ).astype(BF16)
                rs_copy(tick, 0, far, c).start()

            @pl.when((me < n - 1) & (me > near))
            def _():
                rs_copy(tick, 1, near, c).wait_recv()
                part[near, rows(c)] = (
                    part[near, rows(c)].astype(F32) + from_right[tick, near, rows(c)].astype(F32)
                ).astype(BF16)
                rs_copy(tick, 1, near, c).start()

    def rs_drain(tick, c):
        for shard in range(n):
            for way in range(2):
                going = me < shard if way == 0 else me > shard

                @pl.when(going)
                def _():
                    rs_copy(tick, way, shard, c).wait_send()

    def sec_copy(c):
        return pltpu.make_async_remote_copy(
            src_ref=out_ref.at[rows(c)],
            dst_ref=xg.at[1, me, rows(c)],
            send_sem=sec_send.at[c],
            recv_sem=sec_recv.at[c],
            device_id={"section": after},
            device_id_type=MESH,
        )

    def finish(tick, c):
        acc[...] = part[me, rows(c)].astype(F32)

        @pl.when(me > 0)
        def _():
            rs_copy(tick, 0, me, c).wait_recv()
            acc[...] += from_left[tick, me, rows(c)].astype(F32)

        @pl.when(me < n - 1)
        def _():
            rs_copy(tick, 1, me, c).wait_recv()
            acc[...] += from_right[tick, me, rows(c)].astype(F32)

        if tick + 1 == TICKS:
            sec_copy(c).wait_send()
        state = xg[tick, me, rows(c)].astype(F32)
        out_ref[rows(c), :] = (state + gate_ref[me] * acc[...]).astype(BF16)
        if tick + 1 < TICKS:
            sec_copy(c).start()

    def project(tick, c):
        def total(j, sums):
            return sums + jnp.sum(xg[tick, j, rows(c)].astype(F32), axis=-1, keepdims=True)

        center = lax.fori_loop(0, n, total, jnp.zeros((size, 1), F32)) / width

        def spread(j, sums):
            off = xg[tick, j, rows(c)].astype(F32) - center
            return sums + jnp.sum(off * off, axis=-1, keepdims=True)

        varied = lax.fori_loop(0, n, spread, jnp.zeros((size, 1), F32)) / width
        inverse = lax.rsqrt(varied + 1e-06)

        @pl.loop(0, n)
        def _(j):
            off = xg[tick, j, rows(c)].astype(F32) - center
            normed[:, pl.ds(pl.multiple_of(j * share, 128), share)] = (
                off * inverse * (1.0 + scale_ref[j]) + shift_ref[j]
            ).astype(BF16)

        at = pl.ds(tokens + tick * rows_all + c * size, size)

        @pl.loop(0, head_cols // 256)
        def _(h):
            start = pl.multiple_of(h * 256, 256)
            cols = pl.ds(start, 256)
            for kind in range(3):
                fresh = jnp.dot(normed[...], wq[kind, :, cols], preferred_element_type=F32).astype(BF16)
                if kind == 2:
                    vals[at, cols] = fresh
                    continue
                for half in range(2):
                    head = fresh[:, half * HD : (half + 1) * HD].astype(F32)
                    head_at = pl.ds(pl.multiple_of(start + half * HD, HD), HD)
                    if kind == 0:
                        queries[rows(c), head_at] = head_norm(head, qg_ref[...])
                    else:
                        keys[at, head_at] = head_norm(head, kg_ref[...])

    def attend(tick, c):
        count = tokens + (tick + 1) * rows_all

        @pl.loop(0, head_cols // HD)
        def _(h):
            cols = pl.ds(pl.multiple_of(h * HD, HD), HD)
            scores = lax.dot_general(
                queries[rows(c), cols],
                keys[0:count, cols],
                (((1,), (1,)), ((), ())),
                preferred_element_type=F32,
            )
            expon = jnp.exp(scores * HD ** (-0.5)) * mask_ref[tick : tick + 1, 0:count]
            total = jnp.sum(expon, axis=-1, keepdims=True)
            probs = (expon * (1.0 / total)).astype(BF16)
            mixed[:, cols] = jnp.dot(
                probs, vals[0:count, cols], preferred_element_type=F32
            ).astype(BF16)

        @pl.loop(0, n)
        def _(j):
            cols = pl.ds(pl.multiple_of(j * share, 128), share)
            part[j, rows(c)] = jnp.dot(
                mixed[...], wo[:, cols], preferred_element_type=F32
            ).astype(BF16)

    for c in range(CHUNKS):
        ag_own(0, c)
    xg[0, me] = x_ref[...]

    load_kv.wait()
    block = 128

    @pl.loop(0, tokens // block)
    def _(i):
        at = pl.ds(pl.multiple_of(i * block, block), block)
        raw = kvb[at]
        vals[at, :] = raw[:, 1, :]
        cached = raw[:, 0, :].astype(F32)
        for h in range(head_cols // HD):
            cols = slice(h * HD, (h + 1) * HD)
            keys[at, cols] = head_norm(cached[:, cols], kg_ref[...])

    for step in range(1, n):
        for c in range(CHUNKS):
            ag_relay(0, c, step)
            if step == n - 1:
                if c == 0:
                    load_wq.wait()
                    load_wo.wait()
                if c > 0:
                    project(0, c - 1)
    project(0, CHUNKS - 1)

    for i in range(CHUNKS + 4):
        if i < CHUNKS:
            attend(0, i)
            rs_first(0, i)
        if 0 <= i - 1 < CHUNKS:
            rs_rest(0, i - 1)
            finish(0, i - 1)
        if 0 <= i - 2 < CHUNKS:
            sec_copy(i - 2).wait_recv()
            ag_own(1, i - 2)
        if 0 <= i - 3 < CHUNKS:
            for step in range(1, n):
                ag_relay(1, i - 3, step)
        if 0 <= i - 4 < CHUNKS:
            project(1, i - 4)
    for c in range(CHUNKS):
        rs_drain(0, c)
    for i in range(CHUNKS + 1):
        if i < CHUNKS:
            attend(1, i)
            rs_first(1, i)
        if 0 <= i - 1 < CHUNKS:
            rs_rest(1, i - 1)
            finish(1, i - 1)
    for c in range(CHUNKS):
        ag_drain(0, c)
        ag_drain(1, c)
        rs_drain(1, c)


def local(
    inflow,
    w_qkv,
    w_out,
    mod_shift,
    mod_scale,
    mod_gate,
    q_gain,
    k_gain,
    kv_cache,
    patch_id,
    positions,
):
    n = lax.axis_size("tp")
    sections = lax.axis_size("section")
    section_no = lax.axis_index("section")
    width = w_out.shape[2]
    head_cols = w_out.shape[1]
    tokens = kv_cache.shape[1]
    patch_rows, share = inflow.shape[1:]
    span = tokens + TICKS * patch_rows
    token_line = jnp.arange(tokens, dtype=jnp.int32)
    mine = lax.dynamic_index_in_dim(patch_id, section_no, 1, keepdims=False)
    rows_at = jnp.take(positions, mine, axis=0)
    hit = jnp.any(rows_at[:, :, None] == token_line[None, None, :], axis=1)
    kept = 1.0 - hit.astype(jnp.float32)
    kept = jnp.concatenate([kept[0:1], kept[0:1] * kept[1:2]], axis=0)
    mask = jnp.concatenate([kept, jnp.ones((TICKS, span - tokens), jnp.float32)], axis=1)
    vmem = pl.BlockSpec(memory_space=pltpu.VMEM)
    hbm = pl.BlockSpec(memory_space=pl.ANY)
    size = patch_rows // CHUNKS
    dma = pltpu.SemaphoreType.DMA
    flops = 2 * TICKS * patch_rows * (4 * width * head_cols + 2 * span * head_cols)
    result = pl.pallas_call(
        functools.partial(kernel, n, sections),
        out_shape=jax.ShapeDtypeStruct((patch_rows, share), BF16),
        in_specs=[vmem, hbm, hbm, vmem, vmem, vmem, vmem, vmem, hbm, vmem],
        out_specs=vmem,
        scratch_shapes=[
            pltpu.VMEM((TICKS, n, patch_rows, share), BF16),
            pltpu.VMEM((3, width, head_cols), BF16),
            pltpu.VMEM((head_cols, width), BF16),
            pltpu.VMEM((tokens, 2, head_cols), BF16),
            pltpu.VMEM((span, head_cols), BF16),
            pltpu.VMEM((span, head_cols), BF16),
            pltpu.VMEM((size, width), BF16),
            pltpu.VMEM((patch_rows, head_cols), BF16),
            pltpu.VMEM((size, head_cols), BF16),
            pltpu.VMEM((n, patch_rows, share), BF16),
            pltpu.VMEM((TICKS, n, patch_rows, share), BF16),
            pltpu.VMEM((TICKS, n, patch_rows, share), BF16),
            pltpu.VMEM((size, share), F32),
            dma((3,)),
            dma((TICKS, 2, n, CHUNKS)),
            dma((TICKS, n, CHUNKS)),
            dma((TICKS, n, CHUNKS)),
            dma((TICKS, n, CHUNKS)),
            dma((TICKS, n, CHUNKS)),
            dma((CHUNKS,)),
            dma((CHUNKS,)),
        ],
        compiler_params=pltpu.CompilerParams(
            collective_id=0, has_side_effects=True, vmem_limit_bytes=56 * 1024 * 1024
        ),
        cost_estimate=pl.CostEstimate(
            flops=flops, bytes_accessed=16 * 1024 * 1024, transcendentals=4 * patch_rows * span
        ),
    )(
        inflow[0],
        jnp.transpose(w_qkv[0], (1, 0, 2)),
        w_out[0],
        mod_shift.reshape(n, 1, share),
        mod_scale.reshape(n, 1, share),
        mod_gate.reshape(n, 1, share),
        q_gain,
        k_gain,
        kv_cache[0],
        mask,
    )
    return result[None]


def solution(mesh):
    placed = (
        P("section", "cfg", "tp"),
        P("section", None, None, "tp"),
        P("section", "tp", None),
        P("section", None),
        P("section", None),
        P("section", None),
        P("section", None),
        P("section", None),
        P("section", "cfg", None, "tp"),
        P(),
        P(),
    )
    return jax.shard_map(
        local, mesh=mesh, in_specs=placed, out_specs=P("section", "cfg", "tp"), check_vma=False
    )
```

```python
import functools

import jax
import jax.numpy as jnp
from jax import lax
from jax.experimental import pallas as pl
from jax.experimental.pallas import tpu as pltpu
from jax.sharding import PartitionSpec as P

HD = 128
TICKS = 2
CHUNKS = 2
MESH = pl.DeviceIdType.MESH
F32 = jnp.float32
BF16 = jnp.bfloat16


def head_norm(values, gain):
    moment = jnp.mean(values * values, axis=-1, keepdims=True)
    return (values * lax.rsqrt(moment + 1e-06) * gain).astype(BF16)


def kernel(
    n,
    sections,
    x_ref,
    wq_hbm,
    wo_hbm,
    shift_ref,
    scale_ref,
    gate_ref,
    qg_ref,
    kg_ref,
    kv_hbm,
    mask_ref,
    out_ref,
    xg,
    wq,
    wo,
    kvb,
    keys,
    vals,
    normed,
    queries,
    mixed,
    part,
    from_left,
    from_right,
    acc,
    local_sem,
    ag_send,
    ag_recv,
    rs_send,
    rs_left,
    rs_right,
    sec_send,
    sec_recv,
):
    me = lax.axis_index("tp")
    sec = lax.axis_index("section")
    after, before = lax.rem(sec + 1, sections), lax.rem(sec + sections - 1, sections)
    rows_all, share = x_ref.shape
    width = n * share
    tokens = kvb.shape[0]
    head_cols = wo.shape[0]
    size = rows_all // CHUNKS

    load_kv = pltpu.make_async_copy(kv_hbm, kvb, local_sem.at[0])
    load_wq = pltpu.make_async_copy(wq_hbm, wq, local_sem.at[1])
    load_wo = pltpu.make_async_copy(wo_hbm, wo, local_sem.at[2])
    load_kv.start()
    load_wq.start()
    load_wo.start()

    barrier = pltpu.get_barrier_semaphore()
    pl.semaphore_signal(barrier, inc=1, device_id={"section": after}, device_id_type=MESH)
    pl.semaphore_signal(barrier, inc=1, device_id={"section": before}, device_id_type=MESH)

    @pl.when(me > 0)
    def _():
        pl.semaphore_signal(barrier, inc=1, device_id={"tp": me - 1}, device_id_type=MESH)

    @pl.when(me < n - 1)
    def _():
        pl.semaphore_signal(barrier, inc=1, device_id={"tp": me + 1}, device_id_type=MESH)

    pl.semaphore_wait(barrier, 2 + jnp.minimum(me, 1) + jnp.minimum(n - 1 - me, 1))

    def rows(c):
        return pl.ds(c * size, size)

    def ag_copy(tick, way, step, c):
        shard = me - step if way == 0 else me + step
        here = xg.at[tick, shard, rows(c)]
        source = x_ref.at[rows(c)] if tick == 0 and step == 0 else here
        return pltpu.make_async_remote_copy(
            src_ref=source,
            dst_ref=here,
            send_sem=ag_send.at[tick, way, step, c],
            recv_sem=ag_recv.at[tick, shard, c],
            device_id={"tp": me + 1 if way == 0 else me - 1},
            device_id_type=MESH,
        )

    def ag_when(way, step):
        held = me - step >= 0 if way == 0 else me + step <= n - 1
        onward = me < n - 1 if way == 0 else me > 0
        return held, onward

    def ag_own(tick, c):
        for way in range(2):
            _, onward = ag_when(way, 0)

            @pl.when(onward)
            def _():
                ag_copy(tick, way, 0, c).start()

    def ag_relay(tick, c, step):
        for way in range(2):
            held, onward = ag_when(way, step)

            @pl.when(held)
            def _():
                ag_copy(tick, way, step, c).wait_recv()

                @pl.when(onward)
                def _():
                    ag_copy(tick, way, step, c).start()

    def ag_drain(tick, c):
        for step in range(n - 1):
            for way in range(2):
                held, onward = ag_when(way, step)

                @pl.when(held & onward)
                def _():
                    ag_copy(tick, way, step, c).wait_send()

    def rs_copy(tick, way, shard, c):
        landing, sems = (from_left, rs_left) if way == 0 else (from_right, rs_right)
        return pltpu.make_async_remote_copy(
            src_ref=part.at[shard, rows(c)],
            dst_ref=landing.at[tick, shard, rows(c)],
            send_sem=rs_send.at[tick, shard, c],
            recv_sem=sems.at[tick, shard, c],
            device_id={"tp": me + 1 if way == 0 else me - 1},
            device_id_type=MESH,
        )

    def rs_first(tick, c):
        @pl.when(me == 0)
        def _():
            for shard in range(n - 1, 0, -1):
                rs_copy(tick, 0, shard, c).start()

        @pl.when(me == n - 1)
        def _():
            for shard in range(n - 1):
                rs_copy(tick, 1, shard, c).start()

    def rs_rest(tick, c):
        for away in range(n - 1):
            far, near = n - 1 - away, away

            @pl.when((me > 0) & (me < far))
            def _():
                rs_copy(tick, 0, far, c).wait_recv()
                part[far, rows(c)] = (
                    part[far, rows(c)].astype(F32) + from_left[tick, far, rows(c)].astype(F32)
                ).astype(BF16)
                rs_copy(tick, 0, far, c).start()

            @pl.when((me < n - 1) & (me > near))
            def _():
                rs_copy(tick, 1, near, c).wait_recv()
                part[near, rows(c)] = (
                    part[near, rows(c)].astype(F32) + from_right[tick, near, rows(c)].astype(F32)
                ).astype(BF16)
                rs_copy(tick, 1, near, c).start()

    def rs_drain(tick, c):
        for shard in range(n):
            for way in range(2):
                going = me < shard if way == 0 else me > shard

                @pl.when(going)
                def _():
                    rs_copy(tick, way, shard, c).wait_send()

    def sec_copy(c):
        return pltpu.make_async_remote_copy(
            src_ref=out_ref.at[rows(c)],
            dst_ref=xg.at[1, me, rows(c)],
            send_sem=sec_send.at[c],
            recv_sem=sec_recv.at[c],
            device_id={"section": after},
            device_id_type=MESH,
        )

    def finish(tick, c):
        acc[...] = part[me, rows(c)].astype(F32)

        @pl.when(me > 0)
        def _():
            rs_copy(tick, 0, me, c).wait_recv()
            acc[...] += from_left[tick, me, rows(c)].astype(F32)

        @pl.when(me < n - 1)
        def _():
            rs_copy(tick, 1, me, c).wait_recv()
            acc[...] += from_right[tick, me, rows(c)].astype(F32)

        if tick + 1 == TICKS:
            sec_copy(c).wait_send()
        state = xg[tick, me, rows(c)].astype(F32)
        out_ref[rows(c), :] = (state + gate_ref[me] * acc[...]).astype(BF16)
        if tick + 1 < TICKS:
            sec_copy(c).start()

    def project(tick, c):
        def total(j, sums):
            return sums + jnp.sum(xg[tick, j, rows(c)].astype(F32), axis=-1, keepdims=True)

        center = lax.fori_loop(0, n, total, jnp.zeros((size, 1), F32)) / width

        def spread(j, sums):
            off = xg[tick, j, rows(c)].astype(F32) - center
            return sums + jnp.sum(off * off, axis=-1, keepdims=True)

        varied = lax.fori_loop(0, n, spread, jnp.zeros((size, 1), F32)) / width
        inverse = lax.rsqrt(varied + 1e-06)

        @pl.loop(0, n)
        def _(j):
            off = xg[tick, j, rows(c)].astype(F32) - center
            normed[:, pl.ds(pl.multiple_of(j * share, 128), share)] = (
                off * inverse * (1.0 + scale_ref[j]) + shift_ref[j]
            ).astype(BF16)

        at = pl.ds(tokens + tick * rows_all + c * size, size)

        @pl.loop(0, head_cols // 256)
        def _(h):
            start = pl.multiple_of(h * 256, 256)
            cols = pl.ds(start, 256)
            for kind in range(3):
                fresh = jnp.dot(normed[...], wq[kind, :, cols], preferred_element_type=F32).astype(BF16)
                if kind == 2:
                    vals[at, cols] = fresh
                    continue
                for half in range(2):
                    head = fresh[:, half * HD : (half + 1) * HD].astype(F32)
                    head_at = pl.ds(pl.multiple_of(start + half * HD, HD), HD)
                    if kind == 0:
                        queries[rows(c), head_at] = head_norm(head, qg_ref[...])
                    else:
                        keys[at, head_at] = head_norm(head, kg_ref[...])

    def attend(tick, c):
        count = tokens + (tick + 1) * rows_all

        @pl.loop(0, head_cols // HD)
        def _(h):
            cols = pl.ds(pl.multiple_of(h * HD, HD), HD)
            scores = lax.dot_general(
                queries[rows(c), cols],
                keys[0:count, cols],
                (((1,), (1,)), ((), ())),
                preferred_element_type=F32,
            )
            expon = jnp.exp(scores * HD ** (-0.5)) * mask_ref[tick : tick + 1, 0:count]
            total = jnp.sum(expon, axis=-1, keepdims=True)
            probs = (expon * (1.0 / total)).astype(BF16)
            mixed[:, cols] = jnp.dot(
                probs, vals[0:count, cols], preferred_element_type=F32
            ).astype(BF16)

        @pl.loop(0, n)
        def _(j):
            cols = pl.ds(pl.multiple_of(j * share, 128), share)
            part[j, rows(c)] = jnp.dot(
                mixed[...], wo[:, cols], preferred_element_type=F32
            ).astype(BF16)

    for c in range(CHUNKS):
        ag_own(0, c)
    xg[0, me] = x_ref[...]

    load_kv.wait()
    block = 128

    @pl.loop(0, tokens // block)
    def _(i):
        at = pl.ds(pl.multiple_of(i * block, block), block)
        raw = kvb[at]
        vals[at, :] = raw[:, 1, :]
        cached = raw[:, 0, :].astype(F32)
        for h in range(head_cols // HD):
            cols = slice(h * HD, (h + 1) * HD)
            keys[at, cols] = head_norm(cached[:, cols], kg_ref[...])

    for step in range(1, n):
        for c in range(CHUNKS):
            ag_relay(0, c, step)
            if step == n - 1:
                if c == 0:
                    load_wq.wait()
                    load_wo.wait()
                if c > 0:
                    project(0, c - 1)
    project(0, CHUNKS - 1)

    for c in range(CHUNKS):
        attend(0, c)
        rs_first(0, c)
    for c in range(CHUNKS):
        rs_rest(0, c)
    for c in range(CHUNKS):
        finish(0, c)
    for c in range(CHUNKS):
        sec_copy(c).wait_recv()
        ag_own(1, c)
    for step in range(1, n):
        for c in range(CHUNKS):
            ag_relay(1, c, step)
            if step == n - 1 and c > 0:
                project(1, c - 1)
    project(1, CHUNKS - 1)
    for c in range(CHUNKS):
        rs_drain(0, c)
    for c in range(CHUNKS):
        attend(1, c)
        rs_first(1, c)
    for c in range(CHUNKS):
        rs_rest(1, c)
    for c in range(CHUNKS):
        finish(1, c)
    for c in range(CHUNKS):
        ag_drain(0, c)
        ag_drain(1, c)
        rs_drain(1, c)


def local(
    inflow,
    w_qkv,
    w_out,
    mod_shift,
    mod_scale,
    mod_gate,
    q_gain,
    k_gain,
    kv_cache,
    patch_id,
    positions,
):
    n = lax.axis_size("tp")
    sections = lax.axis_size("section")
    section_no = lax.axis_index("section")
    width = w_out.shape[2]
    head_cols = w_out.shape[1]
    tokens = kv_cache.shape[1]
    patch_rows, share = inflow.shape[1:]
    span = tokens + TICKS * patch_rows
    token_line = jnp.arange(tokens, dtype=jnp.int32)
    mine = lax.dynamic_index_in_dim(patch_id, section_no, 1, keepdims=False)
    rows_at = jnp.take(positions, mine, axis=0)
    hit = jnp.any(rows_at[:, :, None] == token_line[None, None, :], axis=1)
    kept = 1.0 - hit.astype(jnp.float32)
    kept = jnp.concatenate([kept[0:1], kept[0:1] * kept[1:2]], axis=0)
    mask = jnp.concatenate([kept, jnp.ones((TICKS, span - tokens), jnp.float32)], axis=1)
    vmem = pl.BlockSpec(memory_space=pltpu.VMEM)
    hbm = pl.BlockSpec(memory_space=pl.ANY)
    size = patch_rows // CHUNKS
    dma = pltpu.SemaphoreType.DMA
    flops = 2 * TICKS * patch_rows * (4 * width * head_cols + 2 * span * head_cols)
    result = pl.pallas_call(
        functools.partial(kernel, n, sections),
        out_shape=jax.ShapeDtypeStruct((patch_rows, share), BF16),
        in_specs=[vmem, hbm, hbm, vmem, vmem, vmem, vmem, vmem, hbm, vmem],
        out_specs=vmem,
        scratch_shapes=[
            pltpu.VMEM((TICKS, n, patch_rows, share), BF16),
            pltpu.VMEM((3, width, head_cols), BF16),
            pltpu.VMEM((head_cols, width), BF16),
            pltpu.VMEM((tokens, 2, head_cols), BF16),
            pltpu.VMEM((span, head_cols), BF16),
            pltpu.VMEM((span, head_cols), BF16),
            pltpu.VMEM((size, width), BF16),
            pltpu.VMEM((patch_rows, head_cols), BF16),
            pltpu.VMEM((size, head_cols), BF16),
            pltpu.VMEM((n, patch_rows, share), BF16),
            pltpu.VMEM((TICKS, n, patch_rows, share), BF16),
            pltpu.VMEM((TICKS, n, patch_rows, share), BF16),
            pltpu.VMEM((size, share), F32),
            dma((3,)),
            dma((TICKS, 2, n, CHUNKS)),
            dma((TICKS, n, CHUNKS)),
            dma((TICKS, n, CHUNKS)),
            dma((TICKS, n, CHUNKS)),
            dma((TICKS, n, CHUNKS)),
            dma((CHUNKS,)),
            dma((CHUNKS,)),
        ],
        compiler_params=pltpu.CompilerParams(
            collective_id=0, has_side_effects=True, vmem_limit_bytes=56 * 1024 * 1024
        ),
        cost_estimate=pl.CostEstimate(
            flops=flops, bytes_accessed=16 * 1024 * 1024, transcendentals=4 * patch_rows * span
        ),
    )(
        inflow[0],
        jnp.transpose(w_qkv[0], (1, 0, 2)),
        w_out[0],
        mod_shift.reshape(n, 1, share),
        mod_scale.reshape(n, 1, share),
        mod_gate.reshape(n, 1, share),
        q_gain,
        k_gain,
        kv_cache[0],
        mask,
    )
    return result[None]


def solution(mesh):
    placed = (
        P("section", "cfg", "tp"),
        P("section", None, None, "tp"),
        P("section", "tp", None),
        P("section", None),
        P("section", None),
        P("section", None),
        P("section", None),
        P("section", None),
        P("section", "cfg", None, "tp"),
        P(),
        P(),
    )
    return jax.shard_map(
        local, mesh=mesh, in_specs=placed, out_specs=P("section", "cfg", "tp"), check_vma=False
    )
```

```python
import functools

import jax
import jax.numpy as jnp
from jax import lax
from jax.experimental import pallas as pl
from jax.experimental.pallas import tpu as pltpu
from jax.sharding import PartitionSpec as P

HD = 128
TICKS = 2
CHUNKS = 2
MESH = pl.DeviceIdType.MESH
F32 = jnp.float32
BF16 = jnp.bfloat16


def head_norm(values, gain):
    moment = jnp.mean(values * values, axis=-1, keepdims=True)
    return (values * lax.rsqrt(moment + 1e-06) * gain).astype(BF16)


def kernel(
    n,
    sections,
    x_ref,
    wq_hbm,
    wo_hbm,
    shift_ref,
    scale_ref,
    gate_ref,
    qg_ref,
    kg_ref,
    kv_hbm,
    mask_ref,
    out_ref,
    xg,
    wq,
    wo,
    kvb,
    keys,
    vals,
    normed,
    queries,
    mixed,
    part,
    from_left,
    from_right,
    acc,
    local_sem,
    ag_send,
    ag_recv,
    rs_send,
    rs_left,
    rs_right,
    sec_send,
    sec_recv,
):
    me = lax.axis_index("tp")
    sec = lax.axis_index("section")
    after, before = lax.rem(sec + 1, sections), lax.rem(sec + sections - 1, sections)
    rows_all, share = x_ref.shape
    width = n * share
    tokens = kvb.shape[0]
    head_cols = wo.shape[0]
    size = rows_all // CHUNKS

    load_kv = pltpu.make_async_copy(kv_hbm, kvb, local_sem.at[0])
    load_wq = pltpu.make_async_copy(wq_hbm, wq, local_sem.at[1])
    load_wo = pltpu.make_async_copy(wo_hbm, wo, local_sem.at[2])
    load_kv.start()
    load_wq.start()
    load_wo.start()

    barrier = pltpu.get_barrier_semaphore()
    pl.semaphore_signal(barrier, inc=1, device_id={"section": after}, device_id_type=MESH)
    pl.semaphore_signal(barrier, inc=1, device_id={"section": before}, device_id_type=MESH)

    @pl.when(me > 0)
    def _():
        pl.semaphore_signal(barrier, inc=1, device_id={"tp": me - 1}, device_id_type=MESH)

    @pl.when(me < n - 1)
    def _():
        pl.semaphore_signal(barrier, inc=1, device_id={"tp": me + 1}, device_id_type=MESH)

    pl.semaphore_wait(barrier, 2 + jnp.minimum(me, 1) + jnp.minimum(n - 1 - me, 1))

    def rows(c):
        return pl.ds(c * size, size)

    def ag_copy(tick, way, step, c):
        shard = me - step if way == 0 else me + step
        here = xg.at[tick, shard, rows(c)]
        source = x_ref.at[rows(c)] if tick == 0 and step == 0 else here
        return pltpu.make_async_remote_copy(
            src_ref=source,
            dst_ref=here,
            send_sem=ag_send.at[tick, way, step, c],
            recv_sem=ag_recv.at[tick, shard, c],
            device_id={"tp": me + 1 if way == 0 else me - 1},
            device_id_type=MESH,
        )

    def ag_when(way, step):
        held = me - step >= 0 if way == 0 else me + step <= n - 1
        onward = me < n - 1 if way == 0 else me > 0
        return held, onward

    def ag_own(tick, c):
        for way in range(2):
            _, onward = ag_when(way, 0)

            @pl.when(onward)
            def _():
                ag_copy(tick, way, 0, c).start()

    def ag_relay(tick, c, step):
        for way in range(2):
            held, onward = ag_when(way, step)

            @pl.when(held)
            def _():
                ag_copy(tick, way, step, c).wait_recv()

                @pl.when(onward)
                def _():
                    ag_copy(tick, way, step, c).start()

    def ag_drain(tick, c):
        for step in range(n - 1):
            for way in range(2):
                held, onward = ag_when(way, step)

                @pl.when(held & onward)
                def _():
                    ag_copy(tick, way, step, c).wait_send()

    def rs_copy(tick, way, shard, c):
        landing, sems = (from_left, rs_left) if way == 0 else (from_right, rs_right)
        return pltpu.make_async_remote_copy(
            src_ref=part.at[shard, rows(c)],
            dst_ref=landing.at[tick, shard, rows(c)],
            send_sem=rs_send.at[tick, shard, c],
            recv_sem=sems.at[tick, shard, c],
            device_id={"tp": me + 1 if way == 0 else me - 1},
            device_id_type=MESH,
        )

    def rs_first(tick, c):
        @pl.when(me == 0)
        def _():
            for shard in range(n - 1, 0, -1):
                rs_copy(tick, 0, shard, c).start()

        @pl.when(me == n - 1)
        def _():
            for shard in range(n - 1):
                rs_copy(tick, 1, shard, c).start()

    def rs_rest(tick, c):
        for away in range(n - 1):
            far, near = n - 1 - away, away

            @pl.when((me > 0) & (me < far))
            def _():
                rs_copy(tick, 0, far, c).wait_recv()
                part[far, rows(c)] = (
                    part[far, rows(c)].astype(F32) + from_left[tick, far, rows(c)].astype(F32)
                ).astype(BF16)
                rs_copy(tick, 0, far, c).start()

            @pl.when((me < n - 1) & (me > near))
            def _():
                rs_copy(tick, 1, near, c).wait_recv()
                part[near, rows(c)] = (
                    part[near, rows(c)].astype(F32) + from_right[tick, near, rows(c)].astype(F32)
                ).astype(BF16)
                rs_copy(tick, 1, near, c).start()

    def rs_drain(tick, c):
        for shard in range(n):
            for way in range(2):
                going = me < shard if way == 0 else me > shard

                @pl.when(going)
                def _():
                    rs_copy(tick, way, shard, c).wait_send()

    def sec_copy(c):
        return pltpu.make_async_remote_copy(
            src_ref=out_ref.at[rows(c)],
            dst_ref=xg.at[1, me, rows(c)],
            send_sem=sec_send.at[c],
            recv_sem=sec_recv.at[c],
            device_id={"section": after},
            device_id_type=MESH,
        )

    def finish(tick, c):
        acc[...] = part[me, rows(c)].astype(F32)

        @pl.when(me > 0)
        def _():
            rs_copy(tick, 0, me, c).wait_recv()
            acc[...] += from_left[tick, me, rows(c)].astype(F32)

        @pl.when(me < n - 1)
        def _():
            rs_copy(tick, 1, me, c).wait_recv()
            acc[...] += from_right[tick, me, rows(c)].astype(F32)

        if tick + 1 == TICKS:
            sec_copy(c).wait_send()
        state = xg[tick, me, rows(c)].astype(F32)
        out_ref[rows(c), :] = (state + gate_ref[me] * acc[...]).astype(BF16)
        if tick + 1 < TICKS:
            sec_copy(c).start()

    def project(tick):
        def total(j, sums):
            return sums + jnp.sum(xg[tick, j, pl.ds(0, rows_all)].astype(F32), axis=-1, keepdims=True)

        center = lax.fori_loop(0, n, total, jnp.zeros((rows_all, 1), F32)) / width

        def spread(j, sums):
            off = xg[tick, j, pl.ds(0, rows_all)].astype(F32) - center
            return sums + jnp.sum(off * off, axis=-1, keepdims=True)

        varied = lax.fori_loop(0, n, spread, jnp.zeros((rows_all, 1), F32)) / width
        inverse = lax.rsqrt(varied + 1e-06)

        @pl.loop(0, n)
        def _(j):
            off = xg[tick, j, pl.ds(0, rows_all)].astype(F32) - center
            normed[:, pl.ds(pl.multiple_of(j * share, 128), share)] = (
                off * inverse * (1.0 + scale_ref[j]) + shift_ref[j]
            ).astype(BF16)

        at = pl.ds(tokens + tick * rows_all, rows_all)

        @pl.loop(0, head_cols // 256)
        def _(h):
            start = pl.multiple_of(h * 256, 256)
            cols = pl.ds(start, 256)
            for kind in range(3):
                fresh = jnp.dot(normed[...], wq[kind, :, cols], preferred_element_type=F32).astype(BF16)
                if kind == 2:
                    vals[at, cols] = fresh
                    continue
                for half in range(2):
                    head = fresh[:, half * HD : (half + 1) * HD].astype(F32)
                    head_at = pl.ds(pl.multiple_of(start + half * HD, HD), HD)
                    if kind == 0:
                        queries[pl.ds(0, rows_all), head_at] = head_norm(head, qg_ref[...])
                    else:
                        keys[at, head_at] = head_norm(head, kg_ref[...])

    def attend(tick, c):
        count = tokens + (tick + 1) * rows_all

        @pl.loop(0, head_cols // HD)
        def _(h):
            cols = pl.ds(pl.multiple_of(h * HD, HD), HD)
            scores = lax.dot_general(
                queries[rows(c), cols],
                keys[0:count, cols],
                (((1,), (1,)), ((), ())),
                preferred_element_type=F32,
            )
            expon = jnp.exp(scores * HD ** (-0.5)) * mask_ref[tick : tick + 1, 0:count]
            total = jnp.sum(expon, axis=-1, keepdims=True)
            probs = (expon * (1.0 / total)).astype(BF16)
            mixed[:, cols] = jnp.dot(
                probs, vals[0:count, cols], preferred_element_type=F32
            ).astype(BF16)

        @pl.loop(0, n)
        def _(j):
            cols = pl.ds(pl.multiple_of(j * share, 128), share)
            part[j, rows(c)] = jnp.dot(
                mixed[...], wo[:, cols], preferred_element_type=F32
            ).astype(BF16)

    for c in range(CHUNKS):
        ag_own(0, c)
    xg[0, me] = x_ref[...]

    load_kv.wait()
    block = 128

    @pl.loop(0, tokens // block)
    def _(i):
        at = pl.ds(pl.multiple_of(i * block, block), block)
        raw = kvb[at]
        vals[at, :] = raw[:, 1, :]
        cached = raw[:, 0, :].astype(F32)
        for h in range(head_cols // HD):
            cols = slice(h * HD, (h + 1) * HD)
            keys[at, cols] = head_norm(cached[:, cols], kg_ref[...])

    for step in range(1, n):
        for c in range(CHUNKS):
            ag_relay(0, c, step)
            if step == n - 1:
                if c == 0:
                    load_wq.wait()
                    load_wo.wait()
    project(0)

    for c in range(CHUNKS):
        attend(0, c)
        rs_first(0, c)
    for c in range(CHUNKS):
        rs_rest(0, c)
    for c in range(CHUNKS):
        finish(0, c)
    for c in range(CHUNKS):
        sec_copy(c).wait_recv()
        ag_own(1, c)
    for step in range(1, n):
        for c in range(CHUNKS):
            ag_relay(1, c, step)
    project(1)
    for c in range(CHUNKS):
        rs_drain(0, c)
    for c in range(CHUNKS):
        attend(1, c)
        rs_first(1, c)
    for c in range(CHUNKS):
        rs_rest(1, c)
    for c in range(CHUNKS):
        finish(1, c)
    for c in range(CHUNKS):
        ag_drain(0, c)
        ag_drain(1, c)
        rs_drain(1, c)


def local(
    inflow,
    w_qkv,
    w_out,
    mod_shift,
    mod_scale,
    mod_gate,
    q_gain,
    k_gain,
    kv_cache,
    patch_id,
    positions,
):
    n = lax.axis_size("tp")
    sections = lax.axis_size("section")
    section_no = lax.axis_index("section")
    width = w_out.shape[2]
    head_cols = w_out.shape[1]
    tokens = kv_cache.shape[1]
    patch_rows, share = inflow.shape[1:]
    span = tokens + TICKS * patch_rows
    token_line = jnp.arange(tokens, dtype=jnp.int32)
    mine = lax.dynamic_index_in_dim(patch_id, section_no, 1, keepdims=False)
    rows_at = jnp.take(positions, mine, axis=0)
    hit = jnp.any(rows_at[:, :, None] == token_line[None, None, :], axis=1)
    kept = 1.0 - hit.astype(jnp.float32)
    kept = jnp.concatenate([kept[0:1], kept[0:1] * kept[1:2]], axis=0)
    mask = jnp.concatenate([kept, jnp.ones((TICKS, span - tokens), jnp.float32)], axis=1)
    vmem = pl.BlockSpec(memory_space=pltpu.VMEM)
    hbm = pl.BlockSpec(memory_space=pl.ANY)
    size = patch_rows // CHUNKS
    dma = pltpu.SemaphoreType.DMA
    flops = 2 * TICKS * patch_rows * (4 * width * head_cols + 2 * span * head_cols)
    result = pl.pallas_call(
        functools.partial(kernel, n, sections),
        out_shape=jax.ShapeDtypeStruct((patch_rows, share), BF16),
        in_specs=[vmem, hbm, hbm, vmem, vmem, vmem, vmem, vmem, hbm, vmem],
        out_specs=vmem,
        scratch_shapes=[
            pltpu.VMEM((TICKS, n, patch_rows, share), BF16),
            pltpu.VMEM((3, width, head_cols), BF16),
            pltpu.VMEM((head_cols, width), BF16),
            pltpu.VMEM((tokens, 2, head_cols), BF16),
            pltpu.VMEM((span, head_cols), BF16),
            pltpu.VMEM((span, head_cols), BF16),
            pltpu.VMEM((patch_rows, width), BF16),
            pltpu.VMEM((patch_rows, head_cols), BF16),
            pltpu.VMEM((size, head_cols), BF16),
            pltpu.VMEM((n, patch_rows, share), BF16),
            pltpu.VMEM((TICKS, n, patch_rows, share), BF16),
            pltpu.VMEM((TICKS, n, patch_rows, share), BF16),
            pltpu.VMEM((size, share), F32),
            dma((3,)),
            dma((TICKS, 2, n, CHUNKS)),
            dma((TICKS, n, CHUNKS)),
            dma((TICKS, n, CHUNKS)),
            dma((TICKS, n, CHUNKS)),
            dma((TICKS, n, CHUNKS)),
            dma((CHUNKS,)),
            dma((CHUNKS,)),
        ],
        compiler_params=pltpu.CompilerParams(
            collective_id=0, has_side_effects=True, vmem_limit_bytes=56 * 1024 * 1024
        ),
        cost_estimate=pl.CostEstimate(
            flops=flops, bytes_accessed=16 * 1024 * 1024, transcendentals=4 * patch_rows * span
        ),
    )(
        inflow[0],
        jnp.transpose(w_qkv[0], (1, 0, 2)),
        w_out[0],
        mod_shift.reshape(n, 1, share),
        mod_scale.reshape(n, 1, share),
        mod_gate.reshape(n, 1, share),
        q_gain,
        k_gain,
        kv_cache[0],
        mask,
    )
    return result[None]


def solution(mesh):
    placed = (
        P("section", "cfg", "tp"),
        P("section", None, None, "tp"),
        P("section", "tp", None),
        P("section", None),
        P("section", None),
        P("section", None),
        P("section", None),
        P("section", None),
        P("section", "cfg", None, "tp"),
        P(),
        P(),
    )
    return jax.shard_map(
        local, mesh=mesh, in_specs=placed, out_specs=P("section", "cfg", "tp"), check_vma=False
    )
```
